768 devices in a mesh: blk: 48 (over y_lo, z, core), grp: 16 (over x, y_hi).
Axes of the slice: x: 4, y: 8 (y_hi: 4, y_lo: 2; y = y_hi * 2 + y_lo), z: 12, core: 2. Of those that a mesh axis runs over, the one named last changes fastest.
Arguments:
- images: bfloat16 [16, 12288, 1152], P('grp', 'blk'), may hold values from -1 to 1
- texts: bfloat16 [16, 12288, 1152], P('grp', 'blk'), may hold values from -1 to 1
- labels: int32 [16, 48, 256], P('grp', 'blk'), may hold values from 0 to 255, each once within a row
- partners: int32 [2, 48], replicated, may hold values from 0 to 47, as said below
- logit_scale: float32 [], replicated, may hold values from 1 to 3
- logit_bias: float32 [], replicated, may hold values from -3 to -1
Outputs:
- image_grad: float32 [16, 12288, 1152], P('grp', 'blk')
- text_grad: float32 [16, 12288, 1152], P('grp', 'blk')
- loss: float32 [], replicated
The draws below stay inside these ranges and needn't reach their ends.
Inputs may be any that keep to these rules, and one draw needn't show every extreme that they name: Each block's labels are a permutation of its 256 text rows. partners[r, i] is block i's partner in round r: partners[r, partners[r, i]] == i and partners[r, i] != i; no two rounds pair the same two blocks.
All inputs are finite; a program needn't handle non-finite values.
Results may differ from the reference program's by a relative error of at most 0.00035.
The reference program's roundings to bfloat16 on the way (of `weight`) count: a program that leaves them out, or rounds other values in their place, can miss the bound.
Values may be sent and summed in bfloat16 or wider, within the bound.
No kernel may reach another device: no remote copies, remote signals or barrier semaphores. Data moves between devices by JAX's collectives and lax.ppermute only.
A program may use at most 32 MiB of HBM per device.

```python
import math
import jax
import jax.numpy as jnp
from jax import lax

D = 1152
ROWS = 256
ROUNDS = 2
BLOCKS = 48
GROUPS = 16
BATCH_G = 12288


def draw_partners(key, part):
    cycle = BLOCKS - 1
    order = jax.random.permutation(jax.random.fold_in(key, 11), BLOCKS).astype(jnp.int32)
    picks = jax.random.permutation(jax.random.fold_in(key, 12), cycle)[:ROUNDS].astype(jnp.int32)
    slots = jnp.arange(BLOCKS, dtype=jnp.int32)

    def one_round(pick):
        other = jnp.where(slots == pick, cycle, (2 * pick - slots) % cycle)
        other = jnp.where(slots == cycle, pick, other).astype(jnp.int32)
        return jnp.zeros((BLOCKS,), jnp.int32).at[order].set(order[other])
    return jax.vmap(one_round)(picks).astype(jnp.int32)


def level_of(key, shape, pieces, least, top_value):
    gain, own = 1.0, jax.random.fold_in(key, 6)
    for position, parts in pieces:
        steps = jnp.exp(jax.random.uniform(jax.random.fold_in(own, position), (parts,), jnp.float32, least / len(pieces), top_value / len(pieces)))
        gain = gain * jnp.repeat(steps, shape[position] // parts).reshape([-1 if axis == position else 1 for axis in range(len(shape))])
    return gain


def gaussian(rng, dims, spread, bound, cuts=(), kind=jnp.bfloat16):
    result = jax.random.normal(rng, dims, jnp.float32) * spread
    if len(cuts) > 0:
        result = level_of(rng, dims, cuts, -0.22, 0.18) * result
    return jnp.clip(result, min=-bound, max=bound).astype(kind)


def setup_inputs(seed: int = 0) -> dict:
    seeds = jax.random.split(jax.random.key(seed), 7)
    images = gaussian(seeds[0], (GROUPS, BATCH_G, D), 0.17, 1.0, ((0, 16), (1, 48)))
    texts = gaussian(seeds[1], (GROUPS, BATCH_G, D), 0.17, 1.0, ((0, 16), (1, 48)))
    labels = jax.vmap(lambda own: jax.random.permutation(own, ROWS))(jax.random.split(seeds[2], GROUPS * BLOCKS)).reshape((GROUPS, BLOCKS, ROWS)).astype(jnp.int32)
    partners = draw_partners(jax.random.fold_in(seeds[6], 71), 0)
    logit_scale = jnp.clip(jnp.exp(jax.random.uniform(seeds[4], (), jnp.float32, math.log(1.0), math.log(3.0))), 1.0, 3.0)
    logit_bias = jnp.clip(jax.random.uniform(seeds[5], (), jnp.float32, -3.0, -1.0), -3.0, -1.0)
    return {"images": images, "texts": texts, "labels": labels, "partners": partners, "logit_scale": logit_scale, "logit_bias": logit_bias}


def pair_terms(image_rows, text_rows, positive, logit_scale, logit_bias):
    logits = logit_scale * jnp.dot(image_rows, text_rows.T, preferred_element_type=jnp.float32) + logit_bias
    signed = jnp.where(positive, jnp.float32(1.0), jnp.float32(-1.0))
    loss_sum = jnp.sum(jax.nn.softplus(-signed * logits))
    weight = (-signed * jax.nn.sigmoid(-signed * logits)).astype(jnp.bfloat16)
    image_part = logit_scale * jnp.dot(weight, text_rows, preferred_element_type=jnp.float32)
    text_part = logit_scale * jnp.dot(weight.T, image_rows, preferred_element_type=jnp.float32)
    return loss_sum, image_part, text_part


def reference(images, texts, labels, partners, logit_scale, logit_bias):
    columns = jnp.arange(ROWS, dtype=jnp.int32)
    nothing = jnp.zeros((ROWS, ROWS), dtype=bool)

    def one_group(operands):
        group_images, group_texts, group_labels = operands
        image_blocks = group_images.reshape(BLOCKS, ROWS, D)
        text_blocks = group_texts.reshape(BLOCKS, ROWS, D)
        positive = group_labels[:, :, None] == columns[None, None, :]
        losses, image_acc, text_acc = lax.map(
            lambda item: pair_terms(item[0], item[1], item[2], logit_scale, logit_bias),
            (image_blocks, text_blocks, positive))
        loss_sum = jnp.sum(losses)
        for round_index in range(ROUNDS):
            partner_row = partners[round_index].astype(jnp.int32)
            cross_loss, cross_image, cross_text = lax.map(
                lambda item: pair_terms(item[0], item[1], nothing, logit_scale, logit_bias),
                (image_blocks, text_blocks[partner_row]))
            loss_sum = loss_sum + jnp.sum(cross_loss)
            image_acc = image_acc + cross_image
            text_acc = text_acc + cross_text[partner_row]
        return loss_sum, image_acc.reshape(BATCH_G, D), text_acc.reshape(BATCH_G, D)

    group_losses, image_grad, text_grad = lax.map(one_group, (images, texts, labels))
    loss = jnp.sum(group_losses) / jnp.float32(GROUPS * BATCH_G)
    return image_grad, text_grad, loss
```

```python
import functools

import jax
import jax.numpy as jnp
from jax import lax
from jax.experimental import pallas as pl
from jax.experimental.pallas import tpu as pltpu
from jax.sharding import Mesh
from jax.sharding import PartitionSpec as P

BLK = ("blk_0", "blk_1", "blk_2")
BLK_GRP = ("blk_0", "blk_1", "blk_2", "grp_0", "grp_1")
GRP = ("grp_0", "grp_1")

PIECE_ROWS = 16
PIECE_COLS = 384
VMEM = pl.BlockSpec(memory_space=pltpu.VMEM)
SMEM = pl.BlockSpec(memory_space=pltpu.SMEM)


def local_kernel(kernel, out_shape, in_specs, out_specs, scratch=(), flops=0, moved=0, exps=0):
    return pl.pallas_call(
        kernel,
        out_shape=out_shape,
        in_specs=in_specs,
        out_specs=out_specs,
        scratch_shapes=list(scratch),
        compiler_params=pltpu.CompilerParams(vmem_limit_bytes=24 << 20),
        cost_estimate=pl.CostEstimate(flops=flops, bytes_accessed=moved, transcendentals=exps),
    )


def piece_at(index, columns):
    row, col = divmod(index, columns // PIECE_COLS)
    return pl.ds(row * PIECE_ROWS, PIECE_ROWS), pl.ds(col * PIECE_COLS, PIECE_COLS)


def pack_kernel(texts, images, packed):
    for index in range(packed.shape[0]):
        rows, cols = piece_at(index, texts.shape[1])
        packed[index, 0] = texts[rows, cols]
        packed[index, 1] = images[rows, cols]


def regroup_kernel(which, partners, spread, send):
    rounds, blocks = partners.shape
    for block in range(blocks):
        for r in range(rounds):
            send[block, r] = spread[partners[r, block], which]


def unpack(received, whole):
    for index in range(received.shape[0]):
        rows, cols = piece_at(index, whole.shape[2])
        for r in range(received.shape[1]):
            whole[r, rows, cols] = received[index, r]


def dot_nt(a, b):
    return lax.dot_general(a, b, (((1,), (1,)), ((), ())), preferred_element_type=jnp.float32)


def dot_tn(a, b):
    return lax.dot_general(a, b, (((0,), (0,)), ((), ())), preferred_element_type=jnp.float32)


def dot_nn(a, b):
    return jnp.dot(a, b, preferred_element_type=jnp.float32)


def sigmoid_parts(x):
    e = jnp.exp(-jnp.abs(x))
    s = 1.0 / (1.0 + e)
    return e, jnp.where(x >= 0, s, e * s)


def own_kernel(scale, bias, images, texts, labels, loss, image_grad, text_grad):
    x, y = images[...], texts[...]
    logits = scale[0, 0] * dot_nt(x, y) + bias[0, 0]
    match = lax.broadcasted_iota(jnp.int32, logits.shape, 1) == labels[...]
    signed = jnp.where(match, -logits, logits)
    e, s = sigmoid_parts(signed)
    loss[0, 0] = jnp.sum(jnp.maximum(signed, 0.0) + jnp.log1p(e))
    weight = jnp.where(match, -s, s).astype(jnp.bfloat16)
    image_grad[...] = scale[0, 0] * dot_nn(weight, y)
    text_grad[...] = scale[0, 0] * dot_tn(weight, x)


def text_kernel(scale, bias, own_loss, images, received, image_part, loss, image_grad, whole):
    unpack(received, whole)
    x = images[...]
    total = own_loss[0, 0]
    grad = image_part[...]
    for r in range(whole.shape[0]):
        logits = scale[0, 0] * dot_nt(x, whole[r]) + bias[0, 0]
        e, s = sigmoid_parts(logits)
        total += jnp.sum(jnp.maximum(logits, 0.0) + jnp.log1p(e))
        grad += scale[0, 0] * dot_nn(s.astype(jnp.bfloat16), whole[r])
    loss[0, 0] = total
    image_grad[...] = grad


def image_kernel(count, scale, bias, loss_sum, texts, received, text_part, loss, text_grad, whole):
    unpack(received, whole)
    y = texts[...]
    grad = text_part[...]
    for r in range(whole.shape[0]):
        logits = scale[0, 0] * dot_nt(y, whole[r]) + bias[0, 0]
        _, s = sigmoid_parts(logits)
        grad += scale[0, 0] * dot_nn(s.astype(jnp.bfloat16), whole[r])
    text_grad[...] = grad
    loss[0, 0] = loss_sum[0, 0] / count


def body(images, texts, labels, partners, logit_scale, logit_bias):
    x, y = images[0], texts[0]
    rows, width = x.shape
    rounds, blocks = partners.shape
    scale, bias = logit_scale.reshape(1, 1), logit_bias.reshape(1, 1)
    piece = (PIECE_ROWS, PIECE_COLS)
    one = jax.ShapeDtypeStruct((1, 1), jnp.float32)
    grad = jax.ShapeDtypeStruct((rows, width), jnp.float32)
    whole = pltpu.VMEM((rounds, rows, width), x.dtype)
    mac = 2 * rows * rows * width
    nbytes = rows * width * 2
    exchange = functools.partial(
        lax.all_to_all, axis_name=BLK, split_axis=0, concat_axis=0, tiled=True
    )

    packed = local_kernel(
        pack_kernel,
        jax.ShapeDtypeStruct((blocks, 2, *piece), x.dtype),
        [VMEM, VMEM],
        VMEM,
        moved=4 * nbytes,
    )(y, x)
    spread = exchange(packed)

    def regroup(which):
        return local_kernel(
            functools.partial(regroup_kernel, which),
            jax.ShapeDtypeStruct((blocks, rounds, *piece), x.dtype),
            [SMEM, VMEM],
            VMEM,
            moved=4 * nbytes,
        )(partners, spread)

    own_loss, image_part, text_part = local_kernel(
        own_kernel,
        (one, grad, grad),
        [SMEM, SMEM, VMEM, VMEM, VMEM],
        (SMEM, VMEM, VMEM),
        flops=3 * mac,
        moved=6 * nbytes,
        exps=3 * rows * rows,
    )(scale, bias, x, y, labels[0].reshape(rows, 1))

    their_texts = exchange(regroup(0))
    send_images, own_loss, image_part, text_part = lax.optimization_barrier(
        (regroup(1), own_loss, image_part, text_part)
    )
    their_images = exchange(send_images)

    loss_part, image_grad = local_kernel(
        text_kernel,
        (one, grad),
        [SMEM, SMEM, SMEM, VMEM, VMEM, VMEM],
        (SMEM, VMEM),
        [whole],
        flops=2 * rounds * mac,
        moved=7 * nbytes,
        exps=3 * rounds * rows * rows,
    )(scale, bias, own_loss, x, their_texts, image_part)
    loss_sum = functools.reduce(lax.psum, BLK_GRP, loss_part)
    count = lax.axis_size(BLK) * lax.axis_size(GRP) * rows
    loss, text_grad = local_kernel(
        functools.partial(image_kernel, float(count)),
        (one, grad),
        [SMEM, SMEM, SMEM, VMEM, VMEM, VMEM],
        (SMEM, VMEM),
        [whole],
        flops=2 * rounds * mac,
        moved=7 * nbytes,
        exps=2 * rounds * rows * rows,
    )(scale, bias, loss_sum, y, their_images, text_part)
    return image_grad[None], text_grad[None], loss[0, 0]


def solution(mesh):
    split = Mesh(
        mesh.devices.reshape(2, 12, 2, 4, 4), ("blk_0", "blk_1", "blk_2", "grp_0", "grp_1")
    )
    in_specs = (P(GRP, BLK, None), P(GRP, BLK, None), P(GRP, BLK, None), P(), P(), P())
    out_specs = (P(GRP, BLK, None), P(GRP, BLK, None), P())
    return jax.shard_map(body, mesh=split, in_specs=in_specs, out_specs=out_specs, check_vma=False)
```

```python
import functools

import jax
import jax.numpy as jnp
from jax import lax
from jax.experimental import pallas as pl
from jax.experimental.pallas import tpu as pltpu
from jax.sharding import Mesh
from jax.sharding import PartitionSpec as P

BLK = ("blk_0", "blk_1", "blk_2")
GRP = ("grp_0", "grp_1")

ROWS = 256
PIECE_ROWS = 16
PIECE_COLS = 384
VMEM = pl.BlockSpec(memory_space=pltpu.VMEM)
SMEM = pl.BlockSpec(memory_space=pltpu.SMEM)
HBM = pl.BlockSpec(memory_space=pltpu.HBM)


def local_kernel(kernel, out_shape, in_specs, out_specs, scratch=(), vmem=24, flops=0, moved=0, exps=0):
    return pl.pallas_call(
        kernel,
        out_shape=out_shape,
        in_specs=in_specs,
        out_specs=out_specs,
        scratch_shapes=list(scratch),
        compiler_params=pltpu.CompilerParams(vmem_limit_bytes=vmem << 20),
        cost_estimate=pl.CostEstimate(flops=flops, bytes_accessed=moved, transcendentals=exps),
    )


def pack_kernel(texts, images, packed, sems):
    row_groups, _, columns = texts.shape
    copies = []
    for which, rows in enumerate((texts, images)):
        for col in range(columns // PIECE_COLS):
            copies.append(
                pltpu.make_async_copy(
                    rows.at[:, :, pl.ds(col * PIECE_COLS, PIECE_COLS)],
                    packed.at[pl.ds(col * row_groups, row_groups), which],
                    sems.at[len(copies)],
                )
            )
    for copy in copies:
        copy.start()
    for copy in copies:
        copy.wait()


def regroup_kernel(which, partners, spread, send):
    rounds, blocks = partners.shape
    for block in range(blocks):
        for r in range(rounds):
            send[block, r] = spread[partners[r, block], which]


def column_group(received, r, col):
    blocks, _, rows, columns = received.shape
    row_groups = ROWS // rows
    return received[pl.ds(col * row_groups, row_groups), r].reshape(ROWS, columns)


def columns_of(col):
    return pl.ds(col * PIECE_COLS, PIECE_COLS)


def dot_nt(a, b):
    return lax.dot_general(a, b, (((1,), (1,)), ((), ())), preferred_element_type=jnp.float32)


def dot_tn(a, b):
    return lax.dot_general(a, b, (((0,), (0,)), ((), ())), preferred_element_type=jnp.float32)


def dot_nn(a, b):
    return jnp.dot(a, b, preferred_element_type=jnp.float32)


def sigmoid_parts(x):
    e = jnp.exp(-jnp.abs(x))
    s = 1.0 / (1.0 + e)
    return e, jnp.where(x >= 0, s, e * s)


def own_kernel(scale, bias, images, texts, labels, loss, image_grad, text_grad):
    x, y = images[...], texts[...]
    logits = scale[0, 0] * dot_nt(x, y) + bias[0, 0]
    match = lax.broadcasted_iota(jnp.int32, logits.shape, 1) == labels[...]
    signed = jnp.where(match, -logits, logits)
    e, s = sigmoid_parts(signed)
    loss[0, 0] = jnp.sum(jnp.maximum(signed, 0.0) + jnp.log1p(e))
    weight = jnp.where(match, -s, s).astype(jnp.bfloat16)
    image_grad[...] = scale[0, 0] * dot_nn(weight, y)
    text_grad[...] = scale[0, 0] * dot_tn(weight, x)


def partner_logits(scale, bias, own, received, r):
    total = jnp.zeros((own.shape[0], own.shape[0]), jnp.float32)
    for col in range(own.shape[1] // PIECE_COLS):
        total += dot_nt(own[:, columns_of(col)], column_group(received, r, col))
    return scale[0, 0] * total + bias[0, 0]


def add_and_write(scale, weights, received, part_copy, acc, grad, sems):
    part_copy.wait()
    copies = []
    for col in range(acc.shape[1] // PIECE_COLS):
        cols = columns_of(col)
        product = sum(
            dot_nn(weight, column_group(received, r, col)) for r, weight in enumerate(weights)
        )
        acc[:, cols] += scale[0, 0] * product
        copy = pltpu.make_async_copy(acc.at[:, cols], grad.at[:, cols], sems.at[col])
        copy.start()
        copies.append(copy)
    for copy in copies:
        copy.wait()


def text_kernel(scale, bias, own_loss, images, received, part, loss, grad, acc, part_sem, sems):
    part_copy = pltpu.make_async_copy(part, acc, part_sem)
    part_copy.start()
    total, weights = own_loss[0, 0], []
    for r in range(received.shape[1]):
        logits = partner_logits(scale, bias, images, received, r)
        e, s = sigmoid_parts(logits)
        total += jnp.sum(jnp.maximum(logits, 0.0) + jnp.log1p(e))
        weights.append(s.astype(jnp.bfloat16))
    loss[0, 0] = total
    add_and_write(scale, weights, received, part_copy, acc, grad, sems)


def image_kernel(scale, bias, texts, received, part, grad, acc, part_sem, sems):
    part_copy = pltpu.make_async_copy(part, acc, part_sem)
    part_copy.start()
    weights = []
    for r in range(received.shape[1]):
        _, s = sigmoid_parts(partner_logits(scale, bias, texts, received, r))
        weights.append(s.astype(jnp.bfloat16))
    add_and_write(scale, weights, received, part_copy, acc, grad, sems)


def shifted(value, axis, by):
    size = lax.axis_size(axis)
    return lax.ppermute(value, axis, [(i, (i + by) % size) for i in range(size)])


def sum_by_pairs(value, axis):
    size, step = lax.axis_size(axis), 1
    while step < size:
        value += lax.ppermute(value, axis, [(i, i ^ step) for i in range(size)])
        step *= 2
    return value


def sum_of_three(a, b, c):
    least, most = jnp.minimum(a, b), jnp.maximum(a, b)
    middle = jnp.maximum(least, jnp.minimum(most, c))
    return (jnp.minimum(least, c) + jnp.maximum(most, c)) + middle


def body(images, texts, labels, partners, logit_scale, logit_bias):
    x, y = images[0], texts[0]
    rows, width = x.shape
    rounds, blocks = partners.shape
    scale, bias = logit_scale.reshape(1, 1), logit_bias.reshape(1, 1)
    piece = (PIECE_ROWS, PIECE_COLS)
    one = jax.ShapeDtypeStruct((1, 1), jnp.float32)
    grad = jax.ShapeDtypeStruct((rows, width), jnp.float32)
    col_groups = width // PIECE_COLS
    scratch = [
        pltpu.VMEM((rows, width), jnp.float32),
        pltpu.SemaphoreType.DMA,
        pltpu.SemaphoreType.DMA((col_groups,)),
    ]
    mac = 2 * rows * rows * width
    nbytes = rows * width * 2
    exchange = functools.partial(
        lax.all_to_all, axis_name=BLK, split_axis=0, concat_axis=0, tiled=True
    )

    packed = local_kernel(
        pack_kernel,
        jax.ShapeDtypeStruct((blocks, 2, *piece), x.dtype),
        [HBM, HBM],
        HBM,
        [pltpu.SemaphoreType.DMA((2 * col_groups,))],
        vmem=60,
        moved=4 * nbytes,
    )(y.reshape(-1, PIECE_ROWS, width), x.reshape(-1, PIECE_ROWS, width))
    spread = exchange(packed)

    def regroup(which):
        return local_kernel(
            functools.partial(regroup_kernel, which),
            jax.ShapeDtypeStruct((blocks, rounds, *piece), x.dtype),
            [SMEM, VMEM],
            VMEM,
            moved=4 * nbytes,
        )(partners, spread)

    own_loss, image_part, text_part = local_kernel(
        own_kernel,
        (one, grad, grad),
        [SMEM, SMEM, VMEM, VMEM, VMEM],
        (SMEM, VMEM, VMEM),
        flops=3 * mac,
        moved=6 * nbytes,
        exps=3 * rows * rows,
    )(scale, bias, x, y, labels[0].reshape(rows, 1))

    their_texts = exchange(regroup(0))
    send_images, own_loss, image_part, text_part = lax.optimization_barrier(
        (regroup(1), own_loss, image_part, text_part)
    )
    their_images = exchange(send_images)

    loss, image_grad = local_kernel(
        text_kernel,
        (one, grad),
        [SMEM, SMEM, SMEM, VMEM, VMEM, HBM],
        (SMEM, HBM),
        scratch,
        vmem=52,
        flops=2 * rounds * mac,
        moved=7 * nbytes,
        exps=3 * rounds * rows * rows,
    )(scale, bias, own_loss, x, their_texts, image_part)
    for axis in ("blk_2", "blk_0", "grp_0", "grp_1"):
        loss = sum_by_pairs(loss, axis)
    loss = (loss + shifted(loss, "blk_1", 6)) + (
        shifted(loss, "blk_1", 3) + shifted(loss, "blk_1", -3)
    )
    their_images, loss = lax.optimization_barrier((their_images, loss))
    loss = sum_of_three(loss, shifted(loss, "blk_1", 1), shifted(loss, "blk_1", -1))
    loss = loss / jnp.float32(lax.axis_size(BLK) * lax.axis_size(GRP) * rows)
    text_grad = local_kernel(
        image_kernel,
        grad,
        [SMEM, SMEM, VMEM, VMEM, HBM],
        HBM,
        scratch,
        vmem=52,
        flops=2 * rounds * mac,
        moved=7 * nbytes,
        exps=2 * rounds * rows * rows,
    )(scale, bias, y, their_images, text_part)
    return image_grad[None], text_grad[None], loss[0, 0]


def solution(mesh):
    split = Mesh(
        mesh.devices.reshape(2, 12, 2, 4, 4), ("blk_0", "blk_1", "blk_2", "grp_0", "grp_1")
    )
    in_specs = (P(GRP, BLK, None), P(GRP, BLK, None), P(GRP, BLK, None), P(), P(), P())
    out_specs = (P(GRP, BLK, None), P(GRP, BLK, None), P())
    return jax.shard_map(body, mesh=split, in_specs=in_specs, out_specs=out_specs, check_vma=False)
```

```python
import functools

import jax
import jax.numpy as jnp
from jax import lax
from jax.experimental import pallas as pl
from jax.experimental.pallas import tpu as pltpu
from jax.sharding import Mesh
from jax.sharding import PartitionSpec as P

BLK = ("blk_0", "blk_1", "blk_2")
GRP = ("grp_0", "grp_1")

ROWS = 256
PIECE_ROWS = 16
PIECE_COLS = 384
VMEM = pl.BlockSpec(memory_space=pltpu.VMEM)
SMEM = pl.BlockSpec(memory_space=pltpu.SMEM)
HBM = pl.BlockSpec(memory_space=pltpu.HBM)


def local_kernel(kernel, out_shape, in_specs, out_specs, scratch=(), vmem=24, flops=0, moved=0, exps=0):
    return pl.pallas_call(
        kernel,
        out_shape=out_shape,
        in_specs=in_specs,
        out_specs=out_specs,
        scratch_shapes=list(scratch),
        compiler_params=pltpu.CompilerParams(vmem_limit_bytes=vmem << 20),
        cost_estimate=pl.CostEstimate(flops=flops, bytes_accessed=moved, transcendentals=exps),
    )


def columns_of(col):
    return pl.ds(col * PIECE_COLS, PIECE_COLS)


def pack_kernel(texts, images, packed, rows, sems):
    copies = [
        pltpu.make_async_copy(block, rows.at[which], sems.at[which])
        for which, block in enumerate((texts, images))
    ]
    for copy in copies:
        copy.start()
    row_groups = ROWS // PIECE_ROWS
    for which, copy in enumerate(copies):
        copy.wait()
        for index in range(packed.shape[0]):
            col, row = divmod(index, row_groups)
            packed[index, which] = rows[which, pl.ds(row * PIECE_ROWS, PIECE_ROWS), columns_of(col)]


def regroup_kernel(which, partners, spread, send):
    rounds, blocks = partners.shape
    for block in range(blocks):
        for r in range(rounds):
            send[block, r] = spread[partners[r, block], which]


def column_group(received, r, col):
    blocks, _, rows, columns = received.shape
    row_groups = ROWS // rows
    return received[pl.ds(col * row_groups, row_groups), r].reshape(ROWS, columns)


def dot_nt(a, b):
    return lax.dot_general(a, b, (((1,), (1,)), ((), ())), preferred_element_type=jnp.float32)


def dot_tn(a, b):
    return lax.dot_general(a, b, (((0,), (0,)), ((), ())), preferred_element_type=jnp.float32)


def dot_nn(a, b):
    return jnp.dot(a, b, preferred_element_type=jnp.float32)


def sigmoid_parts(x):
    e = jnp.exp(-jnp.abs(x))
    s = 1.0 / (1.0 + e)
    return e, jnp.where(x >= 0, s, e * s)


def own_kernel(scale, bias, images, texts, labels, loss, image_grad, text_grad):
    x, y = images[...], texts[...]
    logits = scale[0, 0] * dot_nt(x, y) + bias[0, 0]
    match = lax.broadcasted_iota(jnp.int32, logits.shape, 1) == labels[...]
    signed = jnp.where(match, -logits, logits)
    e, s = sigmoid_parts(signed)
    loss[0, 0] = jnp.sum(jnp.maximum(signed, 0.0) + jnp.log1p(e))
    weight = jnp.where(match, -s, s).astype(jnp.bfloat16)
    image_grad[...] = scale[0, 0] * dot_nn(weight, y)
    text_grad[...] = scale[0, 0] * dot_tn(weight, x)


def partner_logits(scale, bias, own, received, r):
    total = jnp.zeros((own.shape[0], own.shape[0]), jnp.float32)
    for col in range(own.shape[1] // PIECE_COLS):
        total += dot_nt(own[:, columns_of(col)], column_group(received, r, col))
    return scale[0, 0] * total + bias[0, 0]


def add_and_write(scale, weights, received, part_copy, acc, grad, sems):
    part_copy.wait()
    copies = []
    for col in range(acc.shape[1] // PIECE_COLS):
        cols = columns_of(col)
        product = sum(
            dot_nn(weight, column_group(received, r, col)) for r, weight in enumerate(weights)
        )
        acc[:, cols] += scale[0, 0] * product
        copy = pltpu.make_async_copy(acc.at[:, cols], grad.at[:, cols], sems.at[col])
        copy.start()
        copies.append(copy)
    for copy in copies:
        copy.wait()


def loss_kernel(scale, bias, own_loss, images, received, loss, weights):
    total = own_loss[0, 0]
    for r in range(received.shape[1]):
        logits = partner_logits(scale, bias, images, received, r)
        e, s = sigmoid_parts(logits)
        total += jnp.sum(jnp.maximum(logits, 0.0) + jnp.log1p(e))
        weights[r] = s.astype(jnp.bfloat16)
    loss[0, 0] = total


def text_kernel(scale, weights, received, part, grad, acc, part_sem, sems):
    part_copy = pltpu.make_async_copy(part, acc, part_sem)
    part_copy.start()
    weights = [weights[r] for r in range(received.shape[1])]
    add_and_write(scale, weights, received, part_copy, acc, grad, sems)


def image_kernel(scale, bias, texts, received, part, grad, acc, part_sem, sems):
    part_copy = pltpu.make_async_copy(part, acc, part_sem)
    part_copy.start()
    weights = []
    for r in range(received.shape[1]):
        _, s = sigmoid_parts(partner_logits(scale, bias, texts, received, r))
        weights.append(s.astype(jnp.bfloat16))
    add_and_write(scale, weights, received, part_copy, acc, grad, sems)


def body(images, texts, labels, partners, logit_scale, logit_bias):
    x, y = images[0], texts[0]
    rows, width = x.shape
    rounds, blocks = partners.shape
    scale, bias = logit_scale.reshape(1, 1), logit_bias.reshape(1, 1)
    piece = (PIECE_ROWS, PIECE_COLS)
    one = jax.ShapeDtypeStruct((1, 1), jnp.float32)
    grad = jax.ShapeDtypeStruct((rows, width), jnp.float32)
    col_groups = width // PIECE_COLS
    scratch = [
        pltpu.VMEM((rows, width), jnp.float32),
        pltpu.SemaphoreType.DMA,
        pltpu.SemaphoreType.DMA((col_groups,)),
    ]
    mac = 2 * rows * rows * width
    nbytes = rows * width * 2
    exchange = functools.partial(
        lax.all_to_all, axis_name=BLK, split_axis=0, concat_axis=0, tiled=True
    )

    packed = local_kernel(
        pack_kernel,
        jax.ShapeDtypeStruct((blocks, 2, *piece), x.dtype),
        [HBM, HBM],
        VMEM,
        [pltpu.VMEM((2, rows, width), x.dtype), pltpu.SemaphoreType.DMA((2,))],
        vmem=56,
        moved=4 * nbytes,
    )(y, x)
    spread = exchange(packed)

    def regroup(which):
        return local_kernel(
            functools.partial(regroup_kernel, which),
            jax.ShapeDtypeStruct((blocks, rounds, *piece), x.dtype),
            [SMEM, VMEM],
            VMEM,
            moved=4 * nbytes,
        )(partners, spread)

    own_loss, image_part, text_part = local_kernel(
        own_kernel,
        (one, grad, grad),
        [SMEM, SMEM, VMEM, VMEM, VMEM],
        (SMEM, VMEM, VMEM),
        flops=3 * mac,
        moved=6 * nbytes,
        exps=3 * rows * rows,
    )(scale, bias, x, y, labels[0].reshape(rows, 1))

    their_texts = exchange(regroup(0))
    send_images, own_loss, image_part, text_part = lax.optimization_barrier(
        (regroup(1), own_loss, image_part, text_part)
    )
    their_images = exchange(send_images)

    loss, weights = local_kernel(
        loss_kernel,
        (one, jax.ShapeDtypeStruct((rounds, rows, rows), x.dtype)),
        [SMEM, SMEM, SMEM, VMEM, VMEM],
        (SMEM, VMEM),
        flops=rounds * mac,
        moved=3 * nbytes,
        exps=3 * rounds * rows * rows,
    )(scale, bias, own_loss, x, their_texts)
    image_grad = local_kernel(
        text_kernel,
        grad,
        [SMEM, VMEM, VMEM, HBM],
        HBM,
        scratch,
        vmem=52,
        flops=rounds * mac,
        moved=6 * nbytes,
    )(scale, weights, their_texts, image_part)
    for axis in ("blk_2", "blk_0", "grp_0", "grp_1"):
        loss = lax.psum(loss, axis)
    z = lax.axis_size("blk_1")
    loss = jnp.broadcast_to(loss.reshape(1, 1, 1), (z, 1, 128))
    their_images, loss = lax.optimization_barrier((their_images, loss))
    loss = lax.all_to_all(loss, "blk_1", split_axis=0, concat_axis=0, tiled=True)
    loss = jnp.sum(loss[:, :, :1], axis=0)
    loss = loss / jnp.float32(lax.axis_size(BLK) * lax.axis_size(GRP) * rows)
    text_grad = local_kernel(
        image_kernel,
        grad,
        [SMEM, SMEM, VMEM, VMEM, HBM],
        HBM,
        scratch,
        vmem=52,
        flops=2 * rounds * mac,
        moved=7 * nbytes,
        exps=2 * rounds * rows * rows,
    )(scale, bias, y, their_images, text_part)
    return image_grad[None], text_grad[None], loss[0, 0]


def solution(mesh):
    split = Mesh(
        mesh.devices.reshape(2, 12, 2, 4, 4), ("blk_0", "blk_1", "blk_2", "grp_0", "grp_1")
    )
    in_specs = (P(GRP, BLK, None), P(GRP, BLK, None), P(GRP, BLK, None), P(), P(), P())
    out_specs = (P(GRP, BLK, None), P(GRP, BLK, None), P())
    return jax.shard_map(body, mesh=split, in_specs=in_specs, out_specs=out_specs, check_vma=False)
```

```python
import functools

import jax
import jax.numpy as jnp
from jax import lax
from jax.experimental import pallas as pl
from jax.experimental.pallas import tpu as pltpu
from jax.sharding import Mesh
from jax.sharding import PartitionSpec as P

BLK = ("blk_0", "blk_1", "blk_2")
GRP = ("grp_0", "grp_1")

ROWS = 256
PIECE_ROWS = 16
PIECE_COLS = 384
VMEM = pl.BlockSpec(memory_space=pltpu.VMEM)
SMEM = pl.BlockSpec(memory_space=pltpu.SMEM)
HBM = pl.BlockSpec(memory_space=pltpu.HBM)


def local_kernel(kernel, out_shape, in_specs, out_specs, scratch=(), vmem=24, flops=0, moved=0, exps=0):
    return pl.pallas_call(
        kernel,
        out_shape=out_shape,
        in_specs=in_specs,
        out_specs=out_specs,
        scratch_shapes=list(scratch),
        compiler_params=pltpu.CompilerParams(vmem_limit_bytes=vmem << 20),
        cost_estimate=pl.CostEstimate(flops=flops, bytes_accessed=moved, transcendentals=exps),
    )


def columns_of(col):
    return pl.ds(col * PIECE_COLS, PIECE_COLS)


def pack_kernel(texts, images, packed, rows, filled, in_sems, out_sems):
    copies = [
        pltpu.make_async_copy(block, rows.at[which], in_sems.at[which])
        for which, block in enumerate((texts, images))
    ]
    for copy in copies:
        copy.start()
    for copy in copies:
        copy.wait()
    row_groups = ROWS // PIECE_ROWS
    sent = []
    for col in range(packed.shape[0] // row_groups):
        for row in range(row_groups):
            for which in range(len(copies)):
                filled[col * row_groups + row, which] = rows[
                    which, pl.ds(row * PIECE_ROWS, PIECE_ROWS), columns_of(col)
                ]
        part = pl.ds(col * row_groups, row_groups)
        copy = pltpu.make_async_copy(filled.at[part], packed.at[part], out_sems.at[col])
        copy.start()
        sent.append(copy)
    for copy in sent:
        copy.wait()


def regroup_kernel(which, partners, spread, send):
    rounds, blocks = partners.shape
    for block in range(blocks):
        for r in range(rounds):
            send[block, r] = spread[partners[r, block], which]


def column_group(received, r, col):
    blocks, _, rows, columns = received.shape
    row_groups = ROWS // rows
    return received[pl.ds(col * row_groups, row_groups), r].reshape(ROWS, columns)


def dot_nt(a, b):
    return lax.dot_general(a, b, (((1,), (1,)), ((), ())), preferred_element_type=jnp.float32)


def dot_tn(a, b):
    return lax.dot_general(a, b, (((0,), (0,)), ((), ())), preferred_element_type=jnp.float32)


def dot_nn(a, b):
    return jnp.dot(a, b, preferred_element_type=jnp.float32)


def sigmoid_parts(x):
    e = jnp.exp(-jnp.abs(x))
    s = 1.0 / (1.0 + e)
    return e, jnp.where(x >= 0, s, e * s)


def own_kernel(scale, bias, images, texts, labels, loss, image_grad, text_grad):
    x, y = images[...], texts[...]
    logits = scale[0, 0] * dot_nt(x, y) + bias[0, 0]
    match = lax.broadcasted_iota(jnp.int32, logits.shape, 1) == labels[...]
    signed = jnp.where(match, -logits, logits)
    e, s = sigmoid_parts(signed)
    loss[0, 0] = jnp.sum(jnp.maximum(signed, 0.0) + jnp.log1p(e))
    weight = jnp.where(match, -s, s).astype(jnp.bfloat16)
    image_grad[...] = scale[0, 0] * dot_nn(weight, y)
    text_grad[...] = scale[0, 0] * dot_tn(weight, x)


def partner_logits(scale, bias, own, received, r):
    total = jnp.zeros((own.shape[0], own.shape[0]), jnp.float32)
    for col in range(own.shape[1] // PIECE_COLS):
        total += dot_nt(own[:, columns_of(col)], column_group(received, r, col))
    return scale[0, 0] * total + bias[0, 0]


def add_and_write(scale, weights, received, part_copy, acc, grad, sems):
    part_copy.wait()
    copies = []
    for col in range(acc.shape[1] // PIECE_COLS):
        cols = columns_of(col)
        product = sum(
            dot_nn(weight, column_group(received, r, col)) for r, weight in enumerate(weights)
        )
        acc[:, cols] += scale[0, 0] * product
        copy = pltpu.make_async_copy(acc.at[:, cols], grad.at[:, cols], sems.at[col])
        copy.start()
        copies.append(copy)
    for copy in copies:
        copy.wait()


def loss_kernel(scale, bias, own_loss, images, received, loss):
    terms = jnp.zeros((ROWS, ROWS), jnp.float32)
    for r in range(received.shape[1]):
        logits = partner_logits(scale, bias, images, received, r)
        terms += jnp.maximum(logits, 0.0) + jnp.log1p(jnp.exp(-jnp.abs(logits)))
    loss[...] = jnp.full(loss.shape, own_loss[0, 0] + jnp.sum(terms), jnp.float32)


def grad_kernel(scale, bias, own, received, part, grad, acc, part_sem, sems):
    part_copy = pltpu.make_async_copy(part, acc, part_sem)
    part_copy.start()
    weights = []
    for r in range(received.shape[1]):
        _, s = sigmoid_parts(partner_logits(scale, bias, own, received, r))
        weights.append(s.astype(jnp.bfloat16))
    add_and_write(scale, weights, received, part_copy, acc, grad, sems)


def body(images, texts, labels, partners, logit_scale, logit_bias):
    x, y = images[0], texts[0]
    rows, width = x.shape
    rounds, blocks = partners.shape
    scale, bias = logit_scale.reshape(1, 1), logit_bias.reshape(1, 1)
    piece = (PIECE_ROWS, PIECE_COLS)
    one = jax.ShapeDtypeStruct((1, 1), jnp.float32)
    grad = jax.ShapeDtypeStruct((rows, width), jnp.float32)
    col_groups = width // PIECE_COLS
    scratch = [
        pltpu.VMEM((rows, width), jnp.float32),
        pltpu.SemaphoreType.DMA,
        pltpu.SemaphoreType.DMA((col_groups,)),
    ]
    mac = 2 * rows * rows * width
    nbytes = rows * width * 2
    exchange = functools.partial(
        lax.all_to_all, axis_name=BLK, split_axis=0, concat_axis=0, tiled=True
    )

    pieces = jax.ShapeDtypeStruct((blocks, 2, *piece), x.dtype)
    packed = local_kernel(
        pack_kernel,
        pieces,
        [HBM, HBM],
        HBM,
        [
            pltpu.VMEM((2, rows, width), x.dtype),
            pltpu.VMEM(pieces.shape, x.dtype),
            pltpu.SemaphoreType.DMA((2,)),
            pltpu.SemaphoreType.DMA((col_groups,)),
        ],
        vmem=56,
        moved=4 * nbytes,
    )(y, x)
    spread = exchange(packed)

    def regroup(which):
        return local_kernel(
            functools.partial(regroup_kernel, which),
            pieces,
            [SMEM, VMEM],
            VMEM,
            moved=4 * nbytes,
        )(partners, spread)

    own_loss, image_part, text_part = local_kernel(
        own_kernel,
        (one, grad, grad),
        [SMEM, SMEM, VMEM, VMEM, VMEM],
        (SMEM, VMEM, VMEM),
        flops=3 * mac,
        moved=6 * nbytes,
        exps=3 * rows * rows,
    )(scale, bias, x, y, labels[0].reshape(rows, 1))

    their_texts = exchange(regroup(0))
    z = lax.axis_size("blk_1")
    loss = local_kernel(
        loss_kernel,
        jax.ShapeDtypeStruct((z, 1, 128), jnp.float32),
        [SMEM, SMEM, SMEM, VMEM, VMEM],
        VMEM,
        flops=rounds * mac,
        moved=3 * nbytes,
        exps=2 * rounds * rows * rows,
    )(scale, bias, own_loss, x, their_texts)
    loss = lax.all_to_all(loss, "blk_1", split_axis=0, concat_axis=0, tiled=True)
    send_images, loss, image_part, text_part = lax.optimization_barrier(
        (regroup(1), loss, image_part, text_part)
    )
    their_images = exchange(send_images)

    def gradient(own, theirs, part):
        return local_kernel(
            grad_kernel,
            grad,
            [SMEM, SMEM, VMEM, VMEM, HBM],
            HBM,
            scratch,
            vmem=52,
            flops=2 * rounds * mac,
            moved=7 * nbytes,
            exps=2 * rounds * rows * rows,
        )(scale, bias, own, theirs, part)

    image_grad = gradient(x, their_texts, image_part)
    loss = jnp.sum(loss[:, 0, 0])
    for axis in ("blk_2", "blk_0", "grp_0", "grp_1"):
        loss = lax.psum(loss, axis)
    loss = loss / jnp.float32(lax.axis_size(BLK) * lax.axis_size(GRP) * rows)
    their_images, loss, image_grad = lax.optimization_barrier((their_images, loss, image_grad))
    text_grad = gradient(y, their_images, text_part)
    return image_grad[None], text_grad[None], loss


def solution(mesh):
    split = Mesh(
        mesh.devices.reshape(2, 12, 2, 4, 4), ("blk_0", "blk_1", "blk_2", "grp_0", "grp_1")
    )
    in_specs = (P(GRP, BLK, None), P(GRP, BLK, None), P(GRP, BLK, None), P(), P(), P())
    out_specs = (P(GRP, BLK, None), P(GRP, BLK, None), P())
    return jax.shard_map(body, mesh=split, in_specs=in_specs, out_specs=out_specs, check_vma=False)
```

```python
import functools

import jax
import jax.numpy as jnp
from jax import lax
from jax.experimental import pallas as pl
from jax.experimental.pallas import tpu as pltpu
from jax.sharding import Mesh
from jax.sharding import PartitionSpec as P

BLK = ("blk_0", "blk_1", "blk_2")
GRP = ("grp_0", "grp_1")

ROWS = 256
PIECE_ROWS = 16
PIECE_COLS = 384
VMEM = pl.BlockSpec(memory_space=pltpu.VMEM)
SMEM = pl.BlockSpec(memory_space=pltpu.SMEM)
HBM = pl.BlockSpec(memory_space=pltpu.HBM)


def local_kernel(kernel, out_shape, in_specs, out_specs, scratch=(), vmem=24, flops=0, moved=0, exps=0):
    return pl.pallas_call(
        kernel,
        out_shape=out_shape,
        in_specs=in_specs,
        out_specs=out_specs,
        scratch_shapes=list(scratch),
        compiler_params=pltpu.CompilerParams(vmem_limit_bytes=vmem << 20),
        cost_estimate=pl.CostEstimate(flops=flops, bytes_accessed=moved, transcendentals=exps),
    )


def columns_of(col):
    return pl.ds(col * PIECE_COLS, PIECE_COLS)


def pack_kernel(texts, images, packed, rows, filled, in_sems, out_sems):
    copies = [
        pltpu.make_async_copy(block, rows.at[which], in_sems.at[which])
        for which, block in enumerate((texts, images))
    ]
    for copy in copies:
        copy.start()
    for copy in copies:
        copy.wait()
    row_groups = ROWS // PIECE_ROWS
    sent = []
    for col in range(packed.shape[0] // row_groups):
        for row in range(row_groups):
            for which in range(len(copies)):
                filled[col * row_groups + row, which] = rows[
                    which, pl.ds(row * PIECE_ROWS, PIECE_ROWS), columns_of(col)
                ]
        part = pl.ds(col * row_groups, row_groups)
        copy = pltpu.make_async_copy(filled.at[part], packed.at[part], out_sems.at[col])
        copy.start()
        sent.append(copy)
    for copy in sent:
        copy.wait()


def regroup_kernel(which, partners, spread, send):
    rounds, blocks = partners.shape
    for block in range(blocks):
        for r in range(rounds):
            send[block, r] = spread[partners[r, block], which]


def column_group(received, r, col):
    blocks, _, rows, columns = received.shape
    row_groups = ROWS // rows
    return received[pl.ds(col * row_groups, row_groups), r].reshape(ROWS, columns)


def dot_nt(a, b):
    return lax.dot_general(a, b, (((1,), (1,)), ((), ())), preferred_element_type=jnp.float32)


def dot_tn(a, b):
    return lax.dot_general(a, b, (((0,), (0,)), ((), ())), preferred_element_type=jnp.float32)


def dot_nn(a, b):
    return jnp.dot(a, b, preferred_element_type=jnp.float32)


def sigmoid_parts(x):
    e = jnp.exp(-jnp.abs(x))
    s = 1.0 / (1.0 + e)
    return e, jnp.where(x >= 0, s, e * s)


def own_kernel(scale, bias, images, texts, labels, loss, image_grad, text_grad):
    x, y = images[...], texts[...]
    logits = scale[0, 0] * dot_nt(x, y) + bias[0, 0]
    match = lax.broadcasted_iota(jnp.int32, logits.shape, 1) == labels[...]
    signed = jnp.where(match, -logits, logits)
    e, s = sigmoid_parts(signed)
    loss[0, 0] = jnp.sum(jnp.maximum(signed, 0.0) + jnp.log1p(e))
    weight = jnp.where(match, -s, s).astype(jnp.bfloat16)
    image_grad[...] = scale[0, 0] * dot_nn(weight, y)
    text_grad[...] = scale[0, 0] * dot_tn(weight, x)


def partner_logits(scale, bias, own, received, r):
    total = jnp.zeros((own.shape[0], own.shape[0]), jnp.float32)
    for col in range(own.shape[1] // PIECE_COLS):
        total += dot_nt(own[:, columns_of(col)], column_group(received, r, col))
    return scale[0, 0] * total + bias[0, 0]


def add_and_write(scale, weights, received, part_copy, acc, grad, sems):
    part_copy.wait()
    copies = []
    for col in range(acc.shape[1] // PIECE_COLS):
        cols = columns_of(col)
        product = sum(
            dot_nn(weight, column_group(received, r, col)) for r, weight in enumerate(weights)
        )
        acc[:, cols] += scale[0, 0] * product
        copy = pltpu.make_async_copy(acc.at[:, cols], grad.at[:, cols], sems.at[col])
        copy.start()
        copies.append(copy)
    for copy in copies:
        copy.wait()


def loss_kernel(scale, bias, own_loss, images, received, loss):
    terms = jnp.zeros((ROWS, ROWS), jnp.float32)
    for r in range(received.shape[1]):
        logits = partner_logits(scale, bias, images, received, r)
        terms += jnp.maximum(logits, 0.0) + jnp.log1p(jnp.exp(-jnp.abs(logits)))
    loss[0, 0] = own_loss[0, 0] + jnp.sum(terms)


def grad_kernel(scale, bias, own, received, part, grad, acc, part_sem, sems):
    part_copy = pltpu.make_async_copy(part, acc, part_sem)
    part_copy.start()
    weights = []
    for r in range(received.shape[1]):
        _, s = sigmoid_parts(partner_logits(scale, bias, own, received, r))
        weights.append(s.astype(jnp.bfloat16))
    add_and_write(scale, weights, received, part_copy, acc, grad, sems)


def last_kernel(count, a, b, c, *refs):
    operands, loss, rest = refs[:5], refs[5], refs[6:]
    x, y, z = a[0, 0], b[0, 0], c[0, 0]
    least, most = jnp.minimum(x, y), jnp.maximum(x, y)
    middle = jnp.maximum(least, jnp.minimum(most, z))
    loss[0, 0] = ((jnp.minimum(least, z) + jnp.maximum(most, z)) + middle) / count
    grad_kernel(*operands, *rest)


def shifted(value, by):
    size = lax.axis_size("blk_1")
    return lax.ppermute(value, "blk_1", [(i, (i + by) % size) for i in range(size)])


def shifted_beside(value, by):
    size, across = lax.axis_size("blk_1"), lax.axis_size("grp_0")
    pairs = [
        (i * across + j, (i + by) % size * across + (j + 1) % across)
        for i in range(size)
        for j in range(across)
    ]
    return lax.ppermute(value, ("blk_1", "grp_0"), pairs)


def body(images, texts, labels, partners, logit_scale, logit_bias):
    x, y = images[0], texts[0]
    rows, width = x.shape
    rounds, blocks = partners.shape
    scale, bias = logit_scale.reshape(1, 1), logit_bias.reshape(1, 1)
    piece = (PIECE_ROWS, PIECE_COLS)
    one = jax.ShapeDtypeStruct((1, 1), jnp.float32)
    grad = jax.ShapeDtypeStruct((rows, width), jnp.float32)
    col_groups = width // PIECE_COLS
    scratch = [
        pltpu.VMEM((rows, width), jnp.float32),
        pltpu.SemaphoreType.DMA,
        pltpu.SemaphoreType.DMA((col_groups,)),
    ]
    mac = 2 * rows * rows * width
    nbytes = rows * width * 2
    exchange = functools.partial(
        lax.all_to_all, axis_name=BLK, split_axis=0, concat_axis=0, tiled=True
    )

    pieces = jax.ShapeDtypeStruct((blocks, 2, *piece), x.dtype)
    packed = local_kernel(
        pack_kernel,
        pieces,
        [HBM, HBM],
        HBM,
        [
            pltpu.VMEM((2, rows, width), x.dtype),
            pltpu.VMEM(pieces.shape, x.dtype),
            pltpu.SemaphoreType.DMA((2,)),
            pltpu.SemaphoreType.DMA((col_groups,)),
        ],
        vmem=56,
        moved=4 * nbytes,
    )(y, x)
    spread = exchange(packed)

    def regroup(which):
        return local_kernel(
            functools.partial(regroup_kernel, which),
            pieces,
            [SMEM, VMEM],
            VMEM,
            moved=4 * nbytes,
        )(partners, spread)

    own_loss, image_part, text_part = local_kernel(
        own_kernel,
        (one, grad, grad),
        [SMEM, SMEM, VMEM, VMEM, VMEM],
        (SMEM, VMEM, VMEM),
        flops=3 * mac,
        moved=6 * nbytes,
        exps=3 * rows * rows,
    )(scale, bias, x, y, labels[0].reshape(rows, 1))

    their_texts, send_images, own_loss, image_part, text_part = lax.optimization_barrier(
        (exchange(regroup(0)), regroup(1), own_loss, image_part, text_part)
    )
    loss = local_kernel(
        loss_kernel,
        one,
        [SMEM, SMEM, SMEM, VMEM, VMEM],
        SMEM,
        flops=rounds * mac,
        moved=3 * nbytes,
        exps=2 * rounds * rows * rows,
    )(scale, bias, own_loss, x, their_texts)
    loss = (loss + shifted(loss, 6)) + (shifted(loss, 3) + shifted(loss, -3))
    send_images, loss = lax.optimization_barrier((send_images, loss))
    their_images = exchange(send_images)
    for axis in ("grp_0", "grp_1", "blk_0", "blk_2"):
        loss = lax.psum(loss, axis)
    losses = (loss, shifted_beside(loss, 1), shifted_beside(loss, -1))

    def gradient(kernel, more, outs, own, theirs, part):
        return local_kernel(
            kernel,
            (*outs, grad),
            [SMEM] * (len(more) + 2) + [VMEM, VMEM, HBM],
            (*[SMEM] * len(outs), HBM),
            scratch,
            vmem=52,
            flops=2 * rounds * mac,
            moved=7 * nbytes,
            exps=2 * rounds * rows * rows,
        )(*more, scale, bias, own, theirs, part)

    [image_grad] = gradient(grad_kernel, (), (), x, their_texts, image_part)
    their_images, image_grad = lax.optimization_barrier((their_images, image_grad))
    count = lax.axis_size(BLK) * lax.axis_size(GRP) * rows
    loss, text_grad = gradient(
        functools.partial(last_kernel, float(count)), losses, (one,), y, their_images, text_part
    )
    return image_grad[None], text_grad[None], loss[0, 0]


def solution(mesh):
    split = Mesh(
        mesh.devices.reshape(2, 12, 2, 4, 4), ("blk_0", "blk_1", "blk_2", "grp_0", "grp_1")
    )
    in_specs = (P(GRP, BLK, None), P(GRP, BLK, None), P(GRP, BLK, None), P(), P(), P())
    out_specs = (P(GRP, BLK, None), P(GRP, BLK, None), P())
    return jax.shard_map(body, mesh=split, in_specs=in_specs, out_specs=out_specs, check_vma=False)
```

```python
import functools

import jax
import jax.numpy as jnp
from jax import lax
from jax.experimental import pallas as pl
from jax.experimental.pallas import tpu as pltpu
from jax.sharding import Mesh
from jax.sharding import PartitionSpec as P

BLK = ("blk_0", "blk_1", "blk_2")
GRP = ("grp_0", "grp_1")

ROWS = 256
PIECE_ROWS = 16
PIECE_COLS = 384
VMEM = pl.BlockSpec(memory_space=pltpu.VMEM)
SMEM = pl.BlockSpec(memory_space=pltpu.SMEM)
HBM = pl.BlockSpec(memory_space=pltpu.HBM)


def local_kernel(kernel, out_shape, in_specs, out_specs, scratch=(), vmem=24, flops=0, moved=0, exps=0):
    return pl.pallas_call(
        kernel,
        out_shape=out_shape,
        in_specs=in_specs,
        out_specs=out_specs,
        scratch_shapes=list(scratch),
        compiler_params=pltpu.CompilerParams(vmem_limit_bytes=vmem << 20),
        cost_estimate=pl.CostEstimate(flops=flops, bytes_accessed=moved, transcendentals=exps),
    )


def columns_of(col):
    return pl.ds(col * PIECE_COLS, PIECE_COLS)


def pack_kernel(texts, images, packed, rows, filled, in_sems, out_sems):
    copies = [
        pltpu.make_async_copy(block, rows.at[which], in_sems.at[which])
        for which, block in enumerate((texts, images))
    ]
    for copy in copies:
        copy.start()
    row_groups = ROWS // PIECE_ROWS
    sent = []
    for which, copy in enumerate(copies):
        copy.wait()
        for col in range(packed.shape[0] // row_groups):
            for row in range(row_groups):
                filled[col * row_groups + row, which] = rows[
                    which, pl.ds(row * PIECE_ROWS, PIECE_ROWS), columns_of(col)
                ]
            part = pl.ds(col * row_groups, row_groups)
            out = pltpu.make_async_copy(
                filled.at[part, which], packed.at[part, which], out_sems.at[len(sent)]
            )
            out.start()
            sent.append(out)
    for out in sent:
        out.wait()


def regroup_kernel(which, partners, spread, send):
    rounds, blocks = partners.shape
    for block in range(blocks):
        for r in range(rounds):
            send[block, r] = spread[partners[r, block], which]


def column_group(received, r, col):
    blocks, _, rows, columns = received.shape
    row_groups = ROWS // rows
    return received[pl.ds(col * row_groups, row_groups), r].reshape(ROWS, columns)


def dot_nt(a, b):
    return lax.dot_general(a, b, (((1,), (1,)), ((), ())), preferred_element_type=jnp.float32)


def dot_tn(a, b):
    return lax.dot_general(a, b, (((0,), (0,)), ((), ())), preferred_element_type=jnp.float32)


def dot_nn(a, b):
    return jnp.dot(a, b, preferred_element_type=jnp.float32)


def sigmoid_parts(x):
    e = jnp.exp(-jnp.abs(x))
    s = 1.0 / (1.0 + e)
    return e, jnp.where(x >= 0, s, e * s)


def own_kernel(numbers, images, texts, labels, loss, image_grad, text_grad):
    scale, bias = numbers_of(numbers, ROWS)
    x, y = images[...], texts[...]
    logits = scale * dot_nt(x, y) + bias
    match = lax.broadcasted_iota(jnp.int32, logits.shape, 1) == labels[...]
    signed = jnp.where(match, -logits, logits)
    e, s = sigmoid_parts(signed)
    total = jnp.sum(jnp.maximum(signed, 0.0) + jnp.log1p(e))
    loss[...] = jnp.full(loss.shape, total, jnp.float32)
    weight = jnp.where(match, -s, s).astype(jnp.bfloat16)
    scale, _ = numbers_of(numbers, x.shape[1])
    image_grad[...] = scale * dot_nn(weight, y)
    text_grad[...] = scale * dot_tn(weight, x)


def numbers_of(numbers, columns):
    return numbers[0:1, :columns], numbers[1:2, :columns]


def partner_logits(numbers, own, received, r):
    scale, bias = numbers_of(numbers, ROWS)
    total = jnp.zeros((ROWS, ROWS), jnp.float32)
    for col in range(own.shape[1] // PIECE_COLS):
        total += dot_nt(own[:, columns_of(col)], column_group(received, r, col))
    return scale * total + bias


def loss_kernel(numbers, own_loss, images, received, loss):
    terms = jnp.zeros((ROWS, ROWS), jnp.float32)
    for r in range(received.shape[1]):
        logits = partner_logits(numbers, images, received, r)
        terms += jnp.maximum(logits, 0.0) + jnp.log1p(jnp.exp(-jnp.abs(logits)))
    row = own_loss[...] + jnp.sum(terms)
    for place in range(loss.shape[0]):
        loss[place] = row


def grad_kernel(numbers, own, received, part, grad, acc, part_sem, sems):
    part_copy = pltpu.make_async_copy(part, acc, part_sem)
    part_copy.start()
    weights = []
    for r in range(received.shape[1]):
        _, s = sigmoid_parts(partner_logits(numbers, own, received, r))
        weights.append(s.astype(jnp.bfloat16))
    part_copy.wait()
    scale, _ = numbers_of(numbers, PIECE_COLS)
    copies = []
    for col in range(acc.shape[1] // PIECE_COLS):
        cols = columns_of(col)
        product = sum(
            dot_nn(weight, column_group(received, r, col)) for r, weight in enumerate(weights)
        )
        acc[:, cols] += scale * product
        copy = pltpu.make_async_copy(acc.at[:, cols], grad.at[:, cols], sems.at[col])
        copy.start()
        copies.append(copy)
    for copy in copies:
        copy.wait()


def body(images, texts, labels, partners, logit_scale, logit_bias):
    x, y = images[0], texts[0]
    rows, width = x.shape
    rounds, blocks = partners.shape
    numbers = jnp.broadcast_to(jnp.stack([logit_scale, logit_bias])[:, None], (2, width))
    piece = (PIECE_ROWS, PIECE_COLS)
    row = jax.ShapeDtypeStruct((1, 128), jnp.float32)
    grad = jax.ShapeDtypeStruct((rows, width), jnp.float32)
    col_groups = width // PIECE_COLS
    scratch = [
        pltpu.VMEM((rows, width), jnp.float32),
        pltpu.SemaphoreType.DMA,
        pltpu.SemaphoreType.DMA((col_groups,)),
    ]
    mac = 2 * rows * rows * width
    nbytes = rows * width * 2
    exchange = functools.partial(
        lax.all_to_all, axis_name=BLK, split_axis=0, concat_axis=0, tiled=True
    )

    pieces = jax.ShapeDtypeStruct((blocks, 2, *piece), x.dtype)
    packed = local_kernel(
        pack_kernel,
        pieces,
        [HBM, HBM],
        HBM,
        [
            pltpu.VMEM((2, rows, width), x.dtype),
            pltpu.VMEM(pieces.shape, x.dtype),
            pltpu.SemaphoreType.DMA((2,)),
            pltpu.SemaphoreType.DMA((2 * col_groups,)),
        ],
        vmem=56,
        moved=4 * nbytes,
    )(y, x)

    def regroup(which):
        return local_kernel(
            functools.partial(regroup_kernel, which),
            pieces,
            [SMEM, VMEM],
            VMEM,
            moved=4 * nbytes,
        )(partners, spread)

    own_loss, image_part, text_part = local_kernel(
        own_kernel,
        (row, grad, grad),
        [VMEM, VMEM, VMEM, VMEM],
        (VMEM, VMEM, VMEM),
        flops=3 * mac,
        moved=6 * nbytes,
        exps=3 * rows * rows,
    )(numbers, x, y, labels[0].reshape(rows, 1))

    spread, own_loss, image_part, text_part = lax.optimization_barrier(
        (exchange(packed), own_loss, image_part, text_part)
    )
    their_texts = exchange(regroup(0))
    z = lax.axis_size("blk_1")
    loss = local_kernel(
        loss_kernel,
        jax.ShapeDtypeStruct((z, 1, 128), jnp.float32),
        [VMEM, VMEM, VMEM, VMEM],
        VMEM,
        flops=rounds * mac,
        moved=3 * nbytes,
        exps=2 * rounds * rows * rows,
    )(numbers, own_loss, x, their_texts)
    loss = lax.all_to_all(loss, "blk_1", split_axis=0, concat_axis=0, tiled=True)
    send_images, loss = lax.optimization_barrier((regroup(1), loss))
    their_images = exchange(send_images)

    def gradient(own, theirs, part):
        return local_kernel(
            grad_kernel,
            grad,
            [VMEM, VMEM, VMEM, HBM],
            HBM,
            scratch,
            vmem=52,
            flops=2 * rounds * mac,
            moved=7 * nbytes,
            exps=2 * rounds * rows * rows,
        )(numbers, own, theirs, part)

    image_grad = gradient(x, their_texts, image_part)
    loss = jnp.sum(loss[:, 0, 0])
    for axis in ("blk_2", "blk_0", "grp_0", "grp_1"):
        loss = lax.psum(loss, axis)
    loss = loss / jnp.float32(lax.axis_size(BLK) * lax.axis_size(GRP) * rows)
    their_images, loss, image_grad = lax.optimization_barrier((their_images, loss, image_grad))
    text_grad = gradient(y, their_images, text_part)
    return image_grad[None], text_grad[None], loss


def solution(mesh):
    split = Mesh(
        mesh.devices.reshape(2, 12, 2, 4, 4), ("blk_0", "blk_1", "blk_2", "grp_0", "grp_1")
    )
    in_specs = (P(GRP, BLK, None), P(GRP, BLK, None), P(GRP, BLK, None), P(), P(), P())
    out_specs = (P(GRP, BLK, None), P(GRP, BLK, None), P())
    return jax.shard_map(body, mesh=split, in_specs=in_specs, out_specs=out_specs, check_vma=False)
```

```python
import functools

import jax
import jax.numpy as jnp
from jax import lax
from jax.experimental import pallas as pl
from jax.experimental.pallas import tpu as pltpu
from jax.sharding import Mesh
from jax.sharding import PartitionSpec as P

BLK = ("blk_0", "blk_1", "blk_2")
GRP = ("grp_0", "grp_1")

ROWS = 256
PIECE_ROWS = 16
PIECE_COLS = 384
VMEM = pl.BlockSpec(memory_space=pltpu.VMEM)
SMEM = pl.BlockSpec(memory_space=pltpu.SMEM)
HBM = pl.BlockSpec(memory_space=pltpu.HBM)


def local_kernel(kernel, out_shape, in_specs, out_specs, scratch=(), vmem=24, flops=0, moved=0, exps=0):
    return pl.pallas_call(
        kernel,
        out_shape=out_shape,
        in_specs=in_specs,
        out_specs=out_specs,
        scratch_shapes=list(scratch),
        compiler_params=pltpu.CompilerParams(vmem_limit_bytes=vmem << 20),
        cost_estimate=pl.CostEstimate(flops=flops, bytes_accessed=moved, transcendentals=exps),
    )


def columns_of(col):
    return pl.ds(col * PIECE_COLS, PIECE_COLS)


def pack_kernel(texts, images, packed, filled, in_sems, out_sems):
    row_groups, _, columns = texts.shape
    groups = []
    for col in range(columns // PIECE_COLS):
        part = pl.ds(col * row_groups, row_groups)
        coming = [
            pltpu.make_async_copy(
                rows.at[:, :, columns_of(col)], filled.at[part, which], in_sems.at[col, which]
            )
            for which, rows in enumerate((texts, images))
        ]
        for copy in coming:
            copy.start()
        groups.append((part, coming))
    sent = []
    for col, (part, coming) in enumerate(groups):
        for copy in coming:
            copy.wait()
        out = pltpu.make_async_copy(filled.at[part], packed.at[part], out_sems.at[col])
        out.start()
        sent.append(out)
    for out in sent:
        out.wait()


def regroup_kernel(partners, spread, *sends):
    rounds, blocks = partners.shape
    for block in range(blocks):
        for r in range(rounds):
            source = partners[r, block]
            for which, send in enumerate(sends):
                send[block, r] = spread[source, which]


def column_group(received, r, col):
    blocks, _, rows, columns = received.shape
    row_groups = ROWS // rows
    return received[pl.ds(col * row_groups, row_groups), r].reshape(ROWS, columns)


def dot_nt(a, b):
    return lax.dot_general(a, b, (((1,), (1,)), ((), ())), preferred_element_type=jnp.float32)


def dot_tn(a, b):
    return lax.dot_general(a, b, (((0,), (0,)), ((), ())), preferred_element_type=jnp.float32)


def dot_nn(a, b):
    return jnp.dot(a, b, preferred_element_type=jnp.float32)


def sigmoid_parts(x):
    e = jnp.exp(-jnp.abs(x))
    s = 1.0 / (1.0 + e)
    return e, jnp.where(x >= 0, s, e * s)


def own_kernel(numbers, images, texts, labels, loss, image_grad, text_grad):
    scale, bias = numbers_of(numbers, ROWS)
    x, y = images[...], texts[...]
    logits = scale * dot_nt(x, y) + bias
    match = lax.broadcasted_iota(jnp.int32, logits.shape, 1) == labels[...]
    signed = jnp.where(match, -logits, logits)
    e, s = sigmoid_parts(signed)
    total = jnp.sum(jnp.maximum(signed, 0.0) + jnp.log1p(e))
    loss[...] = jnp.full(loss.shape, total, jnp.float32)
    weight = jnp.where(match, -s, s).astype(jnp.bfloat16)
    scale, _ = numbers_of(numbers, x.shape[1])
    image_grad[...] = scale * dot_nn(weight, y)
    text_grad[...] = scale * dot_tn(weight, x)


def numbers_of(numbers, columns):
    return numbers[0:1, :columns], numbers[1:2, :columns]


def partner_logits(numbers, own, received, r):
    scale, bias = numbers_of(numbers, ROWS)
    total = jnp.zeros((ROWS, ROWS), jnp.float32)
    for col in range(own.shape[1] // PIECE_COLS):
        total += dot_nt(own[:, columns_of(col)], column_group(received, r, col))
    return scale * total + bias


def loss_kernel(numbers, own_loss, images, received, loss):
    terms = jnp.zeros((ROWS, ROWS), jnp.float32)
    for r in range(received.shape[1]):
        logits = partner_logits(numbers, images, received, r)
        terms += jnp.maximum(logits, 0.0) + jnp.log1p(jnp.exp(-jnp.abs(logits)))
    row = own_loss[...] + jnp.sum(terms)
    for place in range(loss.shape[0]):
        loss[place] = row


def grad_kernel(numbers, own, received, part, grad, acc, part_sem, sems):
    part_copy = pltpu.make_async_copy(part, acc, part_sem)
    part_copy.start()
    weights = []
    for r in range(received.shape[1]):
        _, s = sigmoid_parts(partner_logits(numbers, own, received, r))
        weights.append(s.astype(jnp.bfloat16))
    part_copy.wait()
    scale, _ = numbers_of(numbers, PIECE_COLS)
    copies = []
    for col in range(acc.shape[1] // PIECE_COLS):
        cols = columns_of(col)
        product = sum(
            dot_nn(weight, column_group(received, r, col)) for r, weight in enumerate(weights)
        )
        acc[:, cols] += scale * product
        copy = pltpu.make_async_copy(acc.at[:, cols], grad.at[:, cols], sems.at[col])
        copy.start()
        copies.append(copy)
    for copy in copies:
        copy.wait()


def body(images, texts, labels, partners, logit_scale, logit_bias):
    x, y = images[0], texts[0]
    rows, width = x.shape
    rounds, blocks = partners.shape
    numbers = jnp.broadcast_to(jnp.stack([logit_scale, logit_bias])[:, None], (2, width))
    piece = (PIECE_ROWS, PIECE_COLS)
    row = jax.ShapeDtypeStruct((1, 128), jnp.float32)
    grad = jax.ShapeDtypeStruct((rows, width), jnp.float32)
    col_groups = width // PIECE_COLS
    scratch = [
        pltpu.VMEM((rows, width), jnp.float32),
        pltpu.SemaphoreType.DMA,
        pltpu.SemaphoreType.DMA((col_groups,)),
    ]
    mac = 2 * rows * rows * width
    nbytes = rows * width * 2
    exchange = functools.partial(
        lax.all_to_all, axis_name=BLK, split_axis=0, concat_axis=0, tiled=True
    )

    pieces = jax.ShapeDtypeStruct((blocks, 2, *piece), x.dtype)
    packed = local_kernel(
        pack_kernel,
        pieces,
        [HBM, HBM],
        HBM,
        [
            pltpu.VMEM(pieces.shape, x.dtype),
            pltpu.SemaphoreType.DMA((col_groups, 2)),
            pltpu.SemaphoreType.DMA((col_groups,)),
        ],
        vmem=56,
        moved=4 * nbytes,
    )(y.reshape(-1, PIECE_ROWS, width), x.reshape(-1, PIECE_ROWS, width))

    own_loss, image_part, text_part = local_kernel(
        own_kernel,
        (row, grad, grad),
        [VMEM, VMEM, VMEM, VMEM],
        (VMEM, VMEM, VMEM),
        flops=3 * mac,
        moved=6 * nbytes,
        exps=3 * rows * rows,
    )(numbers, x, y, labels[0].reshape(rows, 1))

    spread, own_loss, image_part, text_part = lax.optimization_barrier(
        (exchange(packed), own_loss, image_part, text_part)
    )
    send_texts, send_images = local_kernel(
        regroup_kernel,
        (pieces, pieces),
        [SMEM, VMEM],
        (VMEM, VMEM),
        moved=6 * nbytes,
    )(partners, spread)
    their_texts = exchange(send_texts)
    z = lax.axis_size("blk_1")
    loss = local_kernel(
        loss_kernel,
        jax.ShapeDtypeStruct((z, 1, 128), jnp.float32),
        [VMEM, VMEM, VMEM, VMEM],
        VMEM,
        flops=rounds * mac,
        moved=3 * nbytes,
        exps=2 * rounds * rows * rows,
    )(numbers, own_loss, x, their_texts)
    loss = lax.all_to_all(loss, "blk_1", split_axis=0, concat_axis=0, tiled=True)
    send_images, loss, their_texts = lax.optimization_barrier((send_images, loss, their_texts))
    their_images = exchange(send_images)

    def gradient(own, theirs, part):
        return local_kernel(
            grad_kernel,
            grad,
            [VMEM, VMEM, VMEM, HBM],
            HBM,
            scratch,
            vmem=52,
            flops=2 * rounds * mac,
            moved=7 * nbytes,
            exps=2 * rounds * rows * rows,
        )(numbers, own, theirs, part)

    image_grad = gradient(x, their_texts, image_part)
    loss = jnp.sum(loss[:, 0, 0])
    for axis in ("blk_2", "blk_0", "grp_0", "grp_1"):
        loss = lax.psum(loss, axis)
    loss = loss / jnp.float32(lax.axis_size(BLK) * lax.axis_size(GRP) * rows)
    their_images, loss, image_grad = lax.optimization_barrier((their_images, loss, image_grad))
    text_grad = gradient(y, their_images, text_part)
    return image_grad[None], text_grad[None], loss


def solution(mesh):
    split = Mesh(
        mesh.devices.reshape(2, 12, 2, 4, 4), ("blk_0", "blk_1", "blk_2", "grp_0", "grp_1")
    )
    in_specs = (P(GRP, BLK, None), P(GRP, BLK, None), P(GRP, BLK, None), P(), P(), P())
    out_specs = (P(GRP, BLK, None), P(GRP, BLK, None), P())
    return jax.shard_map(body, mesh=split, in_specs=in_specs, out_specs=out_specs, check_vma=False)
```

```python
import functools

import jax
import jax.numpy as jnp
from jax import lax
from jax.experimental import pallas as pl
from jax.experimental.pallas import tpu as pltpu
from jax.sharding import Mesh
from jax.sharding import PartitionSpec as P

BLK = ("blk_0", "blk_1", "blk_2")
GRP = ("grp_0", "grp_1")

ROWS = 256
PIECE_ROWS = 16
PIECE_COLS = 384
VMEM = pl.BlockSpec(memory_space=pltpu.VMEM)
SMEM = pl.BlockSpec(memory_space=pltpu.SMEM)
HBM = pl.BlockSpec(memory_space=pltpu.HBM)


def local_kernel(kernel, out_shape, in_specs, out_specs, scratch=(), vmem=24, flops=0, moved=0, exps=0):
    return pl.pallas_call(
        kernel,
        out_shape=out_shape,
        in_specs=in_specs,
        out_specs=out_specs,
        scratch_shapes=list(scratch),
        compiler_params=pltpu.CompilerParams(vmem_limit_bytes=vmem << 20),
        cost_estimate=pl.CostEstimate(flops=flops, bytes_accessed=moved, transcendentals=exps),
    )


def columns_of(col):
    return pl.ds(col * PIECE_COLS, PIECE_COLS)


def pack_kernel(texts, images, packed, filled, in_sems, out_sems):
    row_groups, _, columns = texts.shape
    groups = []
    for col in range(columns // PIECE_COLS):
        part = pl.ds(col * row_groups, row_groups)
        coming = [
            pltpu.make_async_copy(
                rows.at[:, :, columns_of(col)], filled.at[part, which], in_sems.at[col, which]
            )
            for which, rows in enumerate((texts, images))
        ]
        for copy in coming:
            copy.start()
        groups.append((part, coming))
    sent = []
    for col, (part, coming) in enumerate(groups):
        for copy in coming:
            copy.wait()
        out = pltpu.make_async_copy(filled.at[part], packed.at[part], out_sems.at[col])
        out.start()
        sent.append(out)
    for out in sent:
        out.wait()


def regroup_kernel(partners, spread, *sends):
    rounds, blocks = partners.shape
    for block in range(blocks):
        for r in range(rounds):
            source = partners[r, block]
            for which, send in enumerate(sends):
                send[block, r] = spread[source, which]


def column_group(received, r, col):
    blocks, _, rows, columns = received.shape
    row_groups = ROWS // rows
    return received[pl.ds(col * row_groups, row_groups), r].reshape(ROWS, columns)


def dot_nt(a, b):
    return lax.dot_general(a, b, (((1,), (1,)), ((), ())), preferred_element_type=jnp.float32)


def dot_tn(a, b):
    return lax.dot_general(a, b, (((0,), (0,)), ((), ())), preferred_element_type=jnp.float32)


def dot_nn(a, b):
    return jnp.dot(a, b, preferred_element_type=jnp.float32)


def sigmoid_parts(x):
    e = jnp.exp(-jnp.abs(x))
    s = 1.0 / (1.0 + e)
    return e, jnp.where(x >= 0, s, e * s)


def own_kernel(numbers, images, texts, labels, loss, image_grad, text_grad):
    scale, bias = numbers_of(numbers, ROWS)
    x, y = images[...], texts[...]
    logits = scale * dot_nt(x, y) + bias
    match = lax.broadcasted_iota(jnp.int32, logits.shape, 1) == labels[...]
    signed = jnp.where(match, -logits, logits)
    e, s = sigmoid_parts(signed)
    total = jnp.sum(jnp.maximum(signed, 0.0) + jnp.log1p(e))
    loss[...] = jnp.full(loss.shape, total, jnp.float32)
    weight = jnp.where(match, -s, s).astype(jnp.bfloat16)
    scale, _ = numbers_of(numbers, x.shape[1])
    image_grad[...] = scale * dot_nn(weight, y)
    text_grad[...] = scale * dot_tn(weight, x)


def numbers_of(numbers, columns):
    return numbers[0:1, :columns], numbers[1:2, :columns]


def partner_logits(numbers, own, received, r):
    scale, bias = numbers_of(numbers, ROWS)
    total = jnp.zeros((ROWS, ROWS), jnp.float32)
    for col in range(own.shape[1] // PIECE_COLS):
        total += dot_nt(own[:, columns_of(col)], column_group(received, r, col))
    return scale * total + bias


def loss_kernel(numbers, own_loss, images, received, loss):
    terms = jnp.zeros((ROWS, ROWS), jnp.float32)
    for r in range(received.shape[1]):
        logits = partner_logits(numbers, images, received, r)
        terms += jnp.maximum(logits, 0.0) + jnp.log1p(jnp.exp(-jnp.abs(logits)))
    row = own_loss[...] + jnp.sum(terms)
    for place in range(loss.shape[0]):
        loss[place] = row


def grad_kernel(numbers, own, received, part, grad, acc, part_sem, sems):
    part_copy = pltpu.make_async_copy(part, acc, part_sem)
    part_copy.start()
    weights = []
    for r in range(received.shape[1]):
        _, s = sigmoid_parts(partner_logits(numbers, own, received, r))
        weights.append(s.astype(jnp.bfloat16))
    part_copy.wait()
    scale, _ = numbers_of(numbers, PIECE_COLS)
    copies = []
    for col in range(acc.shape[1] // PIECE_COLS):
        cols = columns_of(col)
        product = sum(
            dot_nn(weight, column_group(received, r, col)) for r, weight in enumerate(weights)
        )
        acc[:, cols] += scale * product
        copy = pltpu.make_async_copy(acc.at[:, cols], grad.at[:, cols], sems.at[col])
        copy.start()
        copies.append(copy)
    for copy in copies:
        copy.wait()


def body(images, texts, labels, partners, logit_scale, logit_bias):
    x, y = images[0], texts[0]
    rows, width = x.shape
    rounds, blocks = partners.shape
    numbers = jnp.broadcast_to(jnp.stack([logit_scale, logit_bias])[:, None], (2, width))
    piece = (PIECE_ROWS, PIECE_COLS)
    row = jax.ShapeDtypeStruct((1, 128), jnp.float32)
    grad = jax.ShapeDtypeStruct((rows, width), jnp.float32)
    col_groups = width // PIECE_COLS
    scratch = [
        pltpu.VMEM((rows, width), jnp.float32),
        pltpu.SemaphoreType.DMA,
        pltpu.SemaphoreType.DMA((col_groups,)),
    ]
    mac = 2 * rows * rows * width
    nbytes = rows * width * 2
    exchange = functools.partial(
        lax.all_to_all, axis_name=BLK, split_axis=0, concat_axis=0, tiled=True
    )

    pieces = jax.ShapeDtypeStruct((blocks, 2, *piece), x.dtype)
    packed = local_kernel(
        pack_kernel,
        pieces,
        [HBM, HBM],
        HBM,
        [
            pltpu.VMEM(pieces.shape, x.dtype),
            pltpu.SemaphoreType.DMA((col_groups, 2)),
            pltpu.SemaphoreType.DMA((col_groups,)),
        ],
        vmem=56,
        moved=4 * nbytes,
    )(y.reshape(-1, PIECE_ROWS, width), x.reshape(-1, PIECE_ROWS, width))

    own_loss, image_part, text_part = local_kernel(
        own_kernel,
        (row, grad, grad),
        [VMEM, VMEM, VMEM, VMEM],
        (VMEM, VMEM, VMEM),
        flops=3 * mac,
        moved=6 * nbytes,
        exps=3 * rows * rows,
    )(numbers, x, y, labels[0].reshape(rows, 1))

    spread, own_loss, image_part, text_part = lax.optimization_barrier(
        (exchange(packed), own_loss, image_part, text_part)
    )
    send_texts, send_images = local_kernel(
        regroup_kernel,
        (pieces, pieces),
        [SMEM, VMEM],
        (VMEM, VMEM),
        moved=6 * nbytes,
    )(partners, spread)
    their_texts = exchange(send_texts)
    z = lax.axis_size("blk_1")
    loss = local_kernel(
        loss_kernel,
        jax.ShapeDtypeStruct((z, 1, 128), jnp.float32),
        [VMEM, VMEM, VMEM, VMEM],
        VMEM,
        flops=rounds * mac,
        moved=3 * nbytes,
        exps=2 * rounds * rows * rows,
    )(numbers, own_loss, x, their_texts)
    their_images = exchange(send_images)

    def gradient(own, theirs, part):
        return local_kernel(
            grad_kernel,
            grad,
            [VMEM, VMEM, VMEM, HBM],
            HBM,
            scratch,
            vmem=52,
            flops=2 * rounds * mac,
            moved=7 * nbytes,
            exps=2 * rounds * rows * rows,
        )(numbers, own, theirs, part)

    image_grad = gradient(x, their_texts, image_part)
    for axis in ("blk_2", "blk_0", "grp_0", "grp_1"):
        loss = lax.psum(loss, axis)
    their_images, loss, image_grad = lax.optimization_barrier((their_images, loss, image_grad))
    loss = lax.all_to_all(loss, "blk_1", split_axis=0, concat_axis=0, tiled=True)
    text_grad = gradient(y, their_images, text_part)
    loss = jnp.sum(loss[:, 0, 0])
    loss = loss / jnp.float32(lax.axis_size(BLK) * lax.axis_size(GRP) * rows)
    return image_grad[None], text_grad[None], loss


def solution(mesh):
    split = Mesh(
        mesh.devices.reshape(2, 12, 2, 4, 4), ("blk_0", "blk_1", "blk_2", "grp_0", "grp_1")
    )
    in_specs = (P(GRP, BLK, None), P(GRP, BLK, None), P(GRP, BLK, None), P(), P(), P())
    out_specs = (P(GRP, BLK, None), P(GRP, BLK, None), P())
    return jax.shard_map(body, mesh=split, in_specs=in_specs, out_specs=out_specs, check_vma=False)
```

```python
import functools

import jax
import jax.numpy as jnp
from jax import lax
from jax.experimental import pallas as pl
from jax.experimental.pallas import tpu as pltpu
from jax.sharding import Mesh
from jax.sharding import PartitionSpec as P

BLK = ("blk_0", "blk_1", "blk_2")
GRP = ("grp_0", "grp_1")

ROWS = 256
PIECE_ROWS = 16
PIECE_COLS = 384
VMEM = pl.BlockSpec(memory_space=pltpu.VMEM)
SMEM = pl.BlockSpec(memory_space=pltpu.SMEM)
HBM = pl.BlockSpec(memory_space=pltpu.HBM)


def local_kernel(kernel, out_shape, in_specs, out_specs, scratch=(), vmem=24, flops=0, moved=0, exps=0):
    return pl.pallas_call(
        kernel,
        out_shape=out_shape,
        in_specs=in_specs,
        out_specs=out_specs,
        scratch_shapes=list(scratch),
        compiler_params=pltpu.CompilerParams(vmem_limit_bytes=vmem << 20),
        cost_estimate=pl.CostEstimate(flops=flops, bytes_accessed=moved, transcendentals=exps),
    )


def columns_of(col):
    return pl.ds(col * PIECE_COLS, PIECE_COLS)


def pack_kernel(texts, images, packed, filled, in_sems, out_sems):
    row_groups, _, columns = texts.shape
    groups = []
    for col in range(columns // PIECE_COLS):
        part = pl.ds(col * row_groups, row_groups)
        coming = [
            pltpu.make_async_copy(
                rows.at[:, :, columns_of(col)], filled.at[part, which], in_sems.at[col, which]
            )
            for which, rows in enumerate((texts, images))
        ]
        for copy in coming:
            copy.start()
        groups.append((part, coming))
    sent = []
    for col, (part, coming) in enumerate(groups):
        for copy in coming:
            copy.wait()
        out = pltpu.make_async_copy(filled.at[part], packed.at[part], out_sems.at[col])
        out.start()
        sent.append(out)
    for out in sent:
        out.wait()


def regroup_kernel(partners, spread, *sends):
    rounds, blocks = partners.shape
    for block in range(blocks):
        for r in range(rounds):
            source = partners[r, block]
            for which, send in enumerate(sends):
                send[block, r] = spread[source, which]


def column_group(received, r, col):
    blocks, _, rows, columns = received.shape
    row_groups = ROWS // rows
    return received[pl.ds(col * row_groups, row_groups), r].reshape(ROWS, columns)


def dot_nt(a, b):
    return lax.dot_general(a, b, (((1,), (1,)), ((), ())), preferred_element_type=jnp.float32)


def dot_tn(a, b):
    return lax.dot_general(a, b, (((0,), (0,)), ((), ())), preferred_element_type=jnp.float32)


def dot_nn(a, b):
    return jnp.dot(a, b, preferred_element_type=jnp.float32)


def sigmoid_parts(x):
    e = jnp.exp(-jnp.abs(x))
    s = 1.0 / (1.0 + e)
    return e, jnp.where(x >= 0, s, e * s)


def own_kernel(numbers, images, texts, labels, loss, image_grad, text_grad):
    scale, bias = numbers_of(numbers, ROWS)
    x, y = images[...], texts[...]
    logits = scale * dot_nt(x, y) + bias
    match = lax.broadcasted_iota(jnp.int32, logits.shape, 1) == labels[...]
    signed = jnp.where(match, -logits, logits)
    e, s = sigmoid_parts(signed)
    total = jnp.sum(jnp.maximum(signed, 0.0) + jnp.log1p(e))
    loss[...] = jnp.full(loss.shape, total, jnp.float32)
    weight = jnp.where(match, -s, s).astype(jnp.bfloat16)
    scale, _ = numbers_of(numbers, x.shape[1])
    image_grad[...] = scale * dot_nn(weight, y)
    text_grad[...] = scale * dot_tn(weight, x)


def numbers_of(numbers, columns):
    return numbers[0:1, :columns], numbers[1:2, :columns]


def partner_logits(numbers, own, received, r):
    scale, bias = numbers_of(numbers, ROWS)
    total = jnp.zeros((ROWS, ROWS), jnp.float32)
    for col in range(own.shape[1] // PIECE_COLS):
        total += dot_nt(own[:, columns_of(col)], column_group(received, r, col))
    return scale * total + bias


def loss_kernel(numbers, own_loss, images, received, loss):
    terms = jnp.zeros((ROWS, ROWS), jnp.float32)
    rounds = received.shape[1]
    for first in range(0, rounds, 2):
        inner = None
        for r in range(first, min(first + 2, rounds)):
            logits = partner_logits(numbers, images, received, r)
            terms += jnp.maximum(logits, 0.0)
            e = jnp.exp(-jnp.abs(logits))
            inner = e if inner is None else inner + e + inner * e
        terms += jnp.log1p(inner)
    row = own_loss[...] + jnp.sum(terms)
    for place in range(loss.shape[0]):
        loss[place] = row


def grad_kernel(numbers, own, received, part, grad, acc, part_sem, sems):
    part_copy = pltpu.make_async_copy(part, acc, part_sem)
    part_copy.start()
    weights = []
    for r in range(received.shape[1]):
        _, s = sigmoid_parts(partner_logits(numbers, own, received, r))
        weights.append(s.astype(jnp.bfloat16))
    part_copy.wait()
    scale, _ = numbers_of(numbers, PIECE_COLS)
    copies = []
    for col in range(acc.shape[1] // PIECE_COLS):
        cols = columns_of(col)
        product = sum(
            dot_nn(weight, column_group(received, r, col)) for r, weight in enumerate(weights)
        )
        acc[:, cols] += scale * product
        copy = pltpu.make_async_copy(acc.at[:, cols], grad.at[:, cols], sems.at[col])
        copy.start()
        copies.append(copy)
    for copy in copies:
        copy.wait()


def body(images, texts, labels, partners, logit_scale, logit_bias):
    x, y = images[0], texts[0]
    rows, width = x.shape
    rounds, blocks = partners.shape
    numbers = jnp.broadcast_to(jnp.stack([logit_scale, logit_bias])[:, None], (2, width))
    piece = (PIECE_ROWS, PIECE_COLS)
    row = jax.ShapeDtypeStruct((1, 128), jnp.float32)
    grad = jax.ShapeDtypeStruct((rows, width), jnp.float32)
    col_groups = width // PIECE_COLS
    scratch = [
        pltpu.VMEM((rows, width), jnp.float32),
        pltpu.SemaphoreType.DMA,
        pltpu.SemaphoreType.DMA((col_groups,)),
    ]
    mac = 2 * rows * rows * width
    nbytes = rows * width * 2
    exchange = functools.partial(
        lax.all_to_all, axis_name=BLK, split_axis=0, concat_axis=0, tiled=True
    )

    pieces = jax.ShapeDtypeStruct((blocks, 2, *piece), x.dtype)
    packed = local_kernel(
        pack_kernel,
        pieces,
        [HBM, HBM],
        HBM,
        [
            pltpu.VMEM(pieces.shape, x.dtype),
            pltpu.SemaphoreType.DMA((col_groups, 2)),
            pltpu.SemaphoreType.DMA((col_groups,)),
        ],
        vmem=56,
        moved=4 * nbytes,
    )(y.reshape(-1, PIECE_ROWS, width), x.reshape(-1, PIECE_ROWS, width))

    own_loss, image_part, text_part = local_kernel(
        own_kernel,
        (row, grad, grad),
        [VMEM, VMEM, VMEM, VMEM],
        (VMEM, VMEM, VMEM),
        flops=3 * mac,
        moved=6 * nbytes,
        exps=3 * rows * rows,
    )(numbers, x, y, labels[0].reshape(rows, 1))

    spread, own_loss, image_part, text_part = lax.optimization_barrier(
        (exchange(packed), own_loss, image_part, text_part)
    )
    send_texts, send_images = local_kernel(
        regroup_kernel,
        (pieces, pieces),
        [SMEM, VMEM],
        (VMEM, VMEM),
        moved=6 * nbytes,
    )(partners, spread)
    their_texts = exchange(send_texts)
    z = lax.axis_size("blk_1")
    loss = local_kernel(
        loss_kernel,
        jax.ShapeDtypeStruct((z, 1, 128), jnp.float32),
        [VMEM, VMEM, VMEM, VMEM],
        VMEM,
        flops=rounds * mac,
        moved=3 * nbytes,
        exps=2 * rounds * rows * rows,
    )(numbers, own_loss, x, their_texts)
    loss = lax.all_to_all(loss, "blk_1", split_axis=0, concat_axis=0, tiled=True)
    send_images, loss, their_texts = lax.optimization_barrier((send_images, loss, their_texts))
    their_images = exchange(send_images)

    def gradient(own, theirs, part):
        return local_kernel(
            grad_kernel,
            grad,
            [VMEM, VMEM, VMEM, HBM],
            HBM,
            scratch,
            vmem=52,
            flops=2 * rounds * mac,
            moved=7 * nbytes,
            exps=2 * rounds * rows * rows,
        )(numbers, own, theirs, part)

    image_grad = gradient(x, their_texts, image_part)
    loss = jnp.sum(loss[:, 0, 0])
    for axis in ("blk_2", "blk_0", "grp_0", "grp_1"):
        loss = lax.psum(loss, axis)
    loss = loss / jnp.float32(lax.axis_size(BLK) * lax.axis_size(GRP) * rows)
    their_images, loss, image_grad = lax.optimization_barrier((their_images, loss, image_grad))
    text_grad = gradient(y, their_images, text_part)
    return image_grad[None], text_grad[None], loss


def solution(mesh):
    split = Mesh(
        mesh.devices.reshape(2, 12, 2, 4, 4), ("blk_0", "blk_1", "blk_2", "grp_0", "grp_1")
    )
    in_specs = (P(GRP, BLK, None), P(GRP, BLK, None), P(GRP, BLK, None), P(), P(), P())
    out_specs = (P(GRP, BLK, None), P(GRP, BLK, None), P())
    return jax.shard_map(body, mesh=split, in_specs=in_specs, out_specs=out_specs, check_vma=False)
```
